1024 devices in a mesh: uly: 8 (over z_lo, core), blk: 32 (over y, x), dp: 4 (over z_hi).
Axes of the slice: x: 4, y: 8, z: 16 (z_hi: 4, z_lo: 4; z = z_hi * 4 + z_lo), core: 2. Of those that a mesh axis runs over, the one named last changes fastest.
Arguments:
- queries: bfloat16 [4, 4096, 3072], P('dp', 'blk', 'uly'), may hold values from -96 to 96
- keys: bfloat16 [4, 4096, 3072], P('dp', 'blk', 'uly'), may hold values from -6 to 6
- values: bfloat16 [4, 4096, 3072], P('dp', 'blk', 'uly'), may hold values from -6 to 6
- block_lists: int32 [4, 24, 64, 16], P('dp', 'uly', 'blk'), may hold values from 0 to 63, as said below
- block_counts: int32 [4, 24, 64], P('dp', 'uly', 'blk'), may hold values from 1 to 16, as said below
- w_out: bfloat16 [3072, 3072], P('uly', 'dp'), may hold values from -0.875 to 0.875
Outputs:
- mixed: bfloat16 [4, 4096, 3072], P(None, ('blk', 'uly'), 'dp')
The draws below stay inside these ranges and needn't reach their ends.
Inputs may be any that keep to these rules, and one draw needn't show every extreme that they name: `block_lists`: entry 0 of every list is the query block's own index; the first block_counts entries of a list are distinct; later entries are padding and carry no meaning. `block_counts`: in every clip and head some query block has all 16 entries live.
All inputs are finite; a program needn't handle non-finite values.
Results may differ from the reference program's by a relative error of at most 0.02.
Values may be sent and summed in bfloat16 or wider, within the bound.
A program may use at most 32 MiB of HBM per device.

```python
import jax
import jax.numpy as jnp
from jax import lax

H = 24
HD = 128
DW = 3072
BLOCK = 64
CLIPS = 4
SEQ = 4096
NBLOCKS = 64
KSEL = 16


def base_keys(key):
    return jnp.clip(jax.random.normal(key, (CLIPS, SEQ, H * HD), jnp.float32), -6.0, 6.0)


def draw_queries(key, part):
    key = jax.random.fold_in(key, 11)
    fresh = jnp.clip(jax.random.normal(key, (CLIPS, SEQ, H * HD), jnp.float32), -6.0, 6.0)
    return fresh.astype(jnp.bfloat16)


def draw_keys(key, part):
    shared = base_keys(key)
    return shared.astype(jnp.bfloat16)


def draw_block_lists(key, part):
    key = jax.random.fold_in(key, 13)
    row_total = CLIPS * H * NBLOCKS
    raw_scores = jax.random.randint(key, (row_total, NBLOCKS - 1), 0, 2 ** 20) * NBLOCKS + jnp.arange(NBLOCKS - 1)
    offsets = jnp.argsort(raw_scores, axis=1)[:, :KSEL - 1] + 1
    own_block = jnp.tile(jnp.arange(NBLOCKS), CLIPS * H)[:, None]
    lists = jnp.concatenate([own_block, (own_block + offsets) % NBLOCKS], axis=1)
    return lists.reshape(CLIPS, H, NBLOCKS, KSEL).astype(jnp.int32)


def draw_block_counts(key, part):
    key = jax.random.fold_in(key, 14)
    lower = jax.random.randint(jax.random.fold_in(key, 1), (CLIPS, H, 1), 1, KSEL + 1)
    spread = jax.random.randint(jax.random.fold_in(key, 2), (CLIPS, H, NBLOCKS), 0, 2 ** 20)
    counts = spread % (KSEL + 1 - lower) + lower
    counts = counts.at[:, :, 0].set(KSEL)
    return counts.astype(jnp.int32)


def block_scale(stream_key, extent, pieces, smallest, high):
    gain, own = 1.0, jax.random.fold_in(stream_key, 6)
    for axis_at, blocks in pieces:
        steps = jnp.exp(jax.random.uniform(jax.random.fold_in(own, axis_at), (blocks,), jnp.float32, smallest / len(pieces), high / len(pieces)))
        gain = gain * jnp.repeat(steps, extent[axis_at] // blocks).reshape([-1 if axis == axis_at else 1 for axis in range(len(extent))])
    return gain


def gaussian(key, shape, scale, reach, shards=(), kind=jnp.bfloat16):
    entries = jax.random.normal(key, shape, jnp.float32) * scale
    if len(shards) > 0:
        entries = block_scale(key, shape, shards, -0.22, 0.18) * entries
    return jnp.clip(entries, min=-reach, max=reach).astype(kind)


def setup_inputs(seed: int = 0) -> dict:
    splits = jax.random.split(jax.random.key(seed), 7)
    return {
        "queries": draw_queries(jax.random.fold_in(splits[6], 71), 0),
        "keys": draw_keys(jax.random.fold_in(splits[6], 71), 0),
        "values": gaussian(splits[2], (CLIPS, SEQ, H * HD), 1.0, 6.0, ((0, 4), (1, 32), (2, 8))),
        "block_lists": draw_block_lists(jax.random.fold_in(splits[6], 71), 0),
        "block_counts": draw_block_counts(jax.random.fold_in(splits[6], 71), 0),
        "w_out": gaussian(splits[5], (H * HD, DW), (H * HD // 64) ** -0.5, 0.875, ((0, 8), (1, 4))),
    }


masked_score = -1.0e30


def attend_head(query_block_tiles, key_blocks, value_blocks, chosen, counts_row):
    block_total = query_block_tiles.shape[0]
    logit_scale_factor = HD ** -0.5
    gathered_key_rows = key_blocks[chosen.astype(jnp.int32)].reshape(block_total, KSEL * BLOCK, HD)
    gathered_value_rows = value_blocks[chosen.astype(jnp.int32)].reshape(block_total, KSEL * BLOCK, HD)
    attention_logits = jnp.einsum("sji,soi->sjo", query_block_tiles.astype(jnp.float32), gathered_key_rows.astype(jnp.float32)) * logit_scale_factor
    usable = jnp.repeat(jnp.arange(KSEL)[None, :] < counts_row[:, None], BLOCK, axis=1)
    peak = jnp.max(jnp.where(usable[:, None, :], attention_logits, masked_score), axis=2, keepdims=True)
    probabilities = jnp.where(usable[:, None, :], jnp.exp(attention_logits - peak), 0.0)
    denom = jnp.sum(probabilities, axis=2)
    lowered_precision = lax.optimization_barrier(probabilities.astype(jnp.bfloat16)).astype(jnp.float32)
    value_mixture = jnp.einsum("yep,ypl->yel", lowered_precision, gathered_value_rows.astype(jnp.float32))
    return value_mixture / denom[:, :, None]


def heads_first(array):
    shaped = array.reshape(CLIPS, NBLOCKS, BLOCK, H, HD).transpose(0, 3, 1, 2, 4)
    return shaped.reshape(CLIPS * H, NBLOCKS, BLOCK, HD)


def attend_item(element):
    return attend_head(element[0], element[1], element[2], element[3], element[4])


def reference(queries, keys, values, block_lists, block_counts, w_out):
    stacked = (heads_first(queries), heads_first(keys), heads_first(values),
               block_lists.reshape(CLIPS * H, NBLOCKS, KSEL), block_counts.reshape(CLIPS * H, NBLOCKS))
    outputs = lax.map(attend_item, stacked)
    attended = outputs.reshape(CLIPS, H, NBLOCKS, BLOCK, HD).transpose(0, 2, 3, 1, 4)
    attended = attended.reshape(CLIPS * SEQ, H * HD).astype(jnp.bfloat16)
    mixed = jnp.dot(attended, w_out, preferred_element_type=jnp.float32)
    return mixed.reshape(CLIPS, SEQ, DW).astype(jnp.bfloat16)
```

```python
import functools
import math

import jax
import jax.numpy as jnp
from jax import lax
from jax.experimental import pallas as pl
from jax.experimental.pallas import tpu as pltpu
from jax.sharding import PartitionSpec as P

HD = 128
BLOCK = 64
X_SIZE = 4
MASKED = -1e30
SCALE = HD**-0.5 * math.log2(math.e)
MESH = pl.DeviceIdType.MESH
F32 = jnp.float32
BF16 = jnp.bfloat16


def fused(
    sizes,
    q_hbm,
    k_hbm,
    v_hbm,
    lists,
    counts,
    w_hbm,
    out,
    q_all,
    t_all,
    t_wide,
    hot,
    k_all,
    v_all,
    v_stage,
    top_now,
    sum_now,
    acc,
    o_own,
    o_out,
    o_in,
    st_out,
    st_in,
    a_out,
    a_all,
    w_all,
    part,
    r_out,
    r_in,
    load_sem,
    kv_send,
    kv_recv,
    q_send,
    q_recv,
    t_send,
    t_recv,
    o_send,
    o_recv,
    st_send,
    st_recv,
    a_send,
    a_recv,
    w_send,
    w_recv,
    r_send,
    r_recv,
):
    nx, ny, nz, nd = sizes
    heads, rows = q_hbm.shape[2] // HD, q_hbm.shape[1]
    take = rows // (2 * nz)
    far = ny // 2
    u, b, d = lax.axis_index("uly"), lax.axis_index("blk"), lax.axis_index("dp")
    z, core = u // 2, u % 2
    y, x = b // nx, b % nx

    def at_y(step):
        return {"blk": lax.rem(y + step + ny, ny) * nx + x}

    def at_x(step):
        return {"blk": y * nx + lax.rem(x + step + nx, nx)}

    def at_z(step):
        return {"uly": lax.rem(z + step + nz, nz) * 2 + core}

    def at_a(flip, step):
        return {
            "uly": z * 2 + lax.rem(core + flip, 2),
            "dp": lax.rem(d + step + nd, nd),
        }

    def send(src, dst, send_sem, recv_sem, device):
        return pltpu.make_async_remote_copy(
            src_ref=src,
            dst_ref=dst,
            send_sem=send_sem,
            recv_sem=recv_sem,
            device_id=device,
            device_id_type=MESH,
        )

    def kv_copy(h, way, step, which):
        buffer = (k_all, v_all)[which]
        old, new = (step - 1, step) if way == 0 else ((ny - step + 1) % ny, ny - step)
        return send(
            buffer.at[h, old],
            buffer.at[h, new],
            kv_send.at[h, way, step - 1, which],
            kv_recv.at[h, new, which],
            at_y(1 - 2 * way),
        )

    def q_copy(h, j):
        return send(
            q_all.at[h, 0], q_all.at[h, j], q_send.at[h, j], q_recv.at[h, j], at_x(j)
        )

    def t_copy(j):
        return send(t_all.at[0], t_all.at[j], t_send.at[j], t_recv.at[j], at_x(j))

    def o_copy(h, j):
        return send(
            o_out.at[h, j], o_in.at[h, j], o_send.at[h, j], o_recv.at[h, j], at_x(-j)
        )

    def st_copy(h, j):
        return send(
            st_out.at[h, j],
            st_in.at[h, j],
            st_send.at[h, j],
            st_recv.at[h, j],
            at_x(-j),
        )

    def a_copy(h, flip, step):
        return send(
            a_out.at[h, lax.rem(core + flip, 2)],
            a_all.at[h, step, :, pl.ds(flip * HD, HD)],
            a_send.at[h, flip, step],
            a_recv.at[h, flip, step],
            at_a(flip, step),
        )

    def w_copy(h):
        return send(
            w_hbm.at[pl.ds(h * HD, HD), :],
            w_all.at[h, pl.ds(HD, HD), :],
            w_send.at[h],
            w_recv.at[h],
            at_a(1, 0),
        )

    def r_copy(j, step):
        return send(
            r_out.at[j, step],
            r_in.at[j, step],
            r_send.at[j, step],
            r_recv.at[j, step],
            at_z(j),
        )

    started = []

    def start(copy):
        copy.start()
        started.append(copy)

    def ways(step):
        pairs = []
        for which in range(2):
            for way in range(2):
                if step < far or which == way:
                    pairs.append((way, which))
        return pairs

    def load(src, dst, sem):
        copy = pltpu.make_async_copy(src, dst, sem)
        copy.start()
        return copy

    load_k = [
        load(k_hbm.at[0, :, pl.ds(h * HD, HD)], k_all.at[h, 0], load_sem.at[0, h])
        for h in range(heads)
    ]
    load_v = [
        load(v_hbm.at[0, :, pl.ds(h * HD, HD)], v_stage.at[h], load_sem.at[1, h])
        for h in range(heads)
    ]
    load_q = [
        load(q_hbm.at[0, :, pl.ds(h * HD, HD)], q_all.at[h, 0], load_sem.at[2, h])
        for h in range(heads)
    ]
    load_w = [
        load(
            w_hbm.at[pl.ds(h * HD, HD), :],
            w_all.at[h, pl.ds(0, HD), :],
            load_sem.at[3, h],
        )
        for h in range(heads)
    ]

    barrier = pltpu.get_barrier_semaphore()
    around = [at_y(1), at_y(-1)]
    around += [at_x(j) for j in range(1, nx)]
    around += [at_a(f, s) for s in range(nd) for f in range(2) if f or s]
    around += [at_z(j) for j in range(1, nz)]
    for device in around:
        pl.semaphore_signal(barrier, inc=1, device_id=device, device_id_type=MESH)

    lane = lax.broadcasted_iota(jnp.int32, (1, HD), 1)
    for h in range(heads):
        for i in range(rows // BLOCK):
            seen = jnp.zeros((1, HD), jnp.int32)
            live = counts[0, h, i]
            for n in range(lists.shape[3]):
                hit = (lane == lists[0, h, i, n]) & (jnp.full((1, HD), n) < live)
                seen = seen | hit.astype(jnp.int32)
            line = h * (rows // BLOCK) + i
            t_all[0, line : line + 1, :] = jnp.where(seen > 0, 0.0, MASKED)

    for copy in load_k:
        copy.wait()
    load_v[0].wait()
    v_all[0, 0] = v_stage[0].T
    load_q[0].wait()
    pl.semaphore_wait(barrier, len(around))

    for way, which in ways(1):
        start(kv_copy(0, way, 1, which))
    for j in range(1, nx):
        start(t_copy(j))
        start(q_copy(0, j))

    row = lax.broadcasted_iota(jnp.int32, (rows, HD), 0)
    column = lax.broadcasted_iota(jnp.int32, (rows, HD), 1)
    per = rows // BLOCK
    for s in range(ny):
        owner = lax.rem(y - s + ny, ny) * nx + x
        hot[s] = jnp.where(column == owner * per + row // BLOCK, 1.0, 0.0).astype(BF16)

    for h in range(1, heads):
        load_v[h].wait()
        v_all[h, 0] = v_stage[h].T
        load_q[h].wait()
        for j in range(1, nx):
            start(q_copy(h, j))
    for h in range(heads):
        start(w_copy(h))

    for j in range(1, nx):
        t_copy(j).wait_recv()
    for h in range(heads):
        for j in range(nx):
            for i in range(per):
                line = h * per + i
                wide = jnp.broadcast_to(t_all[j, line : line + 1, :], (BLOCK, HD))
                t_wide[h, j, i * BLOCK : (i + 1) * BLOCK, :] = wide.astype(BF16)

    def attend(h, slots, first):
        keys = jnp.concatenate(
            [jnp.concatenate([k_all[h, s], hot[s]], axis=1) for s in slots], axis=0
        )
        values = jnp.concatenate([v_all[h, s] for s in slots], axis=1)
        queries = jnp.concatenate(
            [q_all[h].reshape(nx * rows, HD), t_wide[h].reshape(nx * rows, HD)], axis=1
        )
        scores = lax.dot_general(
            keys, queries, (((1,), (1,)), ((), ())), preferred_element_type=F32
        )
        top = jnp.max(scores, axis=0, keepdims=True)
        if not first:
            old = top_now[...]
            top = jnp.maximum(top, old)
        probs = jnp.exp2((scores - top) * SCALE)
        total = jnp.sum(probs, axis=0, keepdims=True)
        mixed = jnp.dot(values, probs.astype(BF16), preferred_element_type=F32)
        if not first:
            fade = jnp.exp2((old - top) * SCALE)
            total = total + sum_now[...] * fade
            mixed = mixed + acc[...] * fade
        top_now[...] = top
        sum_now[...] = total
        acc[...] = mixed

    def share(h):
        for j in range(nx):
            lanes = slice(j * rows, (j + 1) * rows)
            st_out[h, j, 0:1, :] = top_now[:, lanes]
            st_out[h, j, 1:2, :] = sum_now[:, lanes]
            if j == 0:
                o_own[h] = acc[:, lanes]
            else:
                o_out[h, j] = acc[:, lanes].astype(BF16)
                start(st_copy(h, j))
                start(o_copy(h, j))

    def merge(h):
        for j in range(1, nx):
            st_copy(h, j).wait_recv()
        tops = [st_out[h, 0, 0:1, :]] + [st_in[h, j, 0:1, :] for j in range(1, nx)]
        sums = [st_out[h, 0, 1:2, :]] + [st_in[h, j, 1:2, :] for j in range(1, nx)]
        top = functools.reduce(jnp.maximum, tops)
        weights = [jnp.exp2((t - top) * SCALE) for t in tops]
        denom = sum(w * s for w, s in zip(weights, sums))
        total = o_own[h] * weights[0]
        for j in range(1, nx):
            o_copy(h, j).wait_recv()
            total = total + o_in[h, j].astype(F32) * weights[j]
        attended = (total / denom).T.astype(BF16)
        for i in range(2 * nz):
            place = slice(i // 2 * take, (i // 2 + 1) * take)
            a_out[h, i % 2, place, :] = attended[i * take : (i + 1) * take, :]
        for step in range(nd - 1, -1, -1):
            for flip in range(2):
                if flip or step:
                    start(a_copy(h, flip, step))
        a_all[h, 0, :, 0:HD] = a_out[h, core]

    def project(h, steps):
        for step in steps:
            for flip in range(2):
                if flip or step:
                    a_copy(h, flip, step).wait_recv()
        group = len(steps)
        lines = group * nz * take
        rows_in = a_all[h, steps[0] : steps[0] + group].reshape(lines, 2 * HD)
        more = jnp.dot(rows_in, w_all[h], preferred_element_type=F32)
        more = more.reshape(group, nz, take, more.shape[1])
        if h > 0:
            more = more + part[steps[0] : steps[0] + group]
        part[steps[0] : steps[0] + group] = more

    for h in range(heads):
        for j in range(1, nx):
            q_copy(h, j).wait_recv()
        attend(h, [0], True)
        for step in range(1, far):
            for way, which in ways(step):
                kv_copy(h, way, step, which).wait_recv()
                if (way, which) in ways(step + 1):
                    start(kv_copy(h, way, step + 1, which))
            if step == 1 and h + 1 < heads:
                for way, which in ways(1):
                    start(kv_copy(h + 1, way, 1, which))
            attend(h, [step, ny - step], False)
            if step == max(1, far - 2) and h > 0:
                merge(h - 1)
            if h == 2 and step == far - 1:
                for i in range(heads):
                    load_w[i].wait()
                    w_copy(i).wait_recv()
                project(0, list(range(nd)))
        for way, which in ways(far):
            kv_copy(h, way, far, which).wait_recv()
        attend(h, [far], False)
        share(h)

    last = heads - 1
    merge(last)
    for h in range(1, last):
        project(h, list(range(nd)))
    for step in range(nd):
        project(last, [step])
        for j in range(1, nz):
            goal = lax.rem(z + j, nz)
            r_out[j, step] = part[step, goal].astype(BF16)
            start(r_copy(j, step))
    for step in range(nd):
        total = part[step, z]
        for j in range(1, nz):
            r_copy(j, step).wait_recv()
            total = total + r_in[j, step].astype(F32)
        out[lax.rem(d - step + nd, nd)] = total.astype(BF16)

    for copy in started:
        copy.wait_send()


def on_device(sizes, queries, keys, values, block_lists, block_counts, w_out):
    nx, ny, nz, nd = sizes
    rows, heads = queries.shape[1], queries.shape[2] // HD
    take, width = rows // (2 * nz), w_out.shape[1]
    dma = pltpu.SemaphoreType.DMA
    far = ny // 2
    return pl.pallas_call(
        functools.partial(fused, sizes),
        out_shape=jax.ShapeDtypeStruct((nd, take, width), BF16),
        in_specs=[pl.BlockSpec(memory_space=pl.ANY)] * 3
        + [pl.BlockSpec(memory_space=pltpu.SMEM)] * 2
        + [pl.BlockSpec(memory_space=pl.ANY)],
        out_specs=pl.BlockSpec(memory_space=pltpu.VMEM),
        scratch_shapes=[
            pltpu.VMEM((heads, nx, rows, HD), BF16),
            pltpu.VMEM((nx, 8, HD), F32),
            pltpu.VMEM((heads, nx, rows, HD), BF16),
            pltpu.VMEM((ny, rows, HD), BF16),
            pltpu.VMEM((heads, ny, rows, HD), BF16),
            pltpu.VMEM((heads, ny, HD, rows), BF16),
            pltpu.VMEM((heads, rows, HD), BF16),
            pltpu.VMEM((1, nx * rows), F32),
            pltpu.VMEM((1, nx * rows), F32),
            pltpu.VMEM((HD, nx * rows), F32),
            pltpu.VMEM((heads, HD, rows), F32),
            pltpu.VMEM((heads, nx, HD, rows), BF16),
            pltpu.VMEM((heads, nx, HD, rows), BF16),
            pltpu.VMEM((heads, nx, 8, rows), F32),
            pltpu.VMEM((heads, nx, 8, rows), F32),
            pltpu.VMEM((heads, 2, nz * take, HD), BF16),
            pltpu.VMEM((heads, nd, nz * take, 2 * HD), BF16),
            pltpu.VMEM((heads, 2 * HD, width), BF16),
            pltpu.VMEM((nd, nz, take, width), F32),
            pltpu.VMEM((nz, nd, take, width), BF16),
            pltpu.VMEM((nz, nd, take, width), BF16),
            dma((4, heads)),
            dma((heads, 2, far, 2)),
            dma((heads, ny, 2)),
            dma((heads, nx)),
            dma((heads, nx)),
            dma((nx,)),
            dma((nx,)),
            dma((heads, nx)),
            dma((heads, nx)),
            dma((heads, nx)),
            dma((heads, nx)),
            dma((heads, 2, nd)),
            dma((heads, 2, nd)),
            dma((heads,)),
            dma((heads,)),
            dma((nz, nd)),
            dma((nz, nd)),
        ],
        compiler_params=pltpu.CompilerParams(
            collective_id=0, has_side_effects=True, vmem_limit_bytes=40 * 2**20
        ),
        name="attention",
    )(queries, keys, values, block_lists, block_counts, w_out)


def solution(mesh):
    shape = mesh.shape
    sizes = (X_SIZE, shape["blk"] // X_SIZE, shape["uly"] // 2, shape["dp"])
    placed = (
        P("dp", "blk", "uly"),
        P("dp", "blk", "uly"),
        P("dp", "blk", "uly"),
        P("dp", "uly", "blk", None),
        P("dp", "uly", "blk"),
        P("uly", "dp"),
    )
    return jax.shard_map(
        functools.partial(on_device, sizes),
        mesh=mesh,
        in_specs=placed,
        out_specs=P(None, ("blk", "uly"), "dp"),
        check_vma=False,
    )
```

```python
import functools
import math

import jax
import jax.numpy as jnp
from jax import lax
from jax.experimental import pallas as pl
from jax.experimental.pallas import tpu as pltpu
from jax.sharding import PartitionSpec as P

HD = 128
BLOCK = 64
X_SIZE = 4
MASKED = -1e30
SCALE = HD**-0.5 * math.log2(math.e)
MESH = pl.DeviceIdType.MESH
F32 = jnp.float32
BF16 = jnp.bfloat16


def fused(
    sizes,
    q_hbm,
    k_hbm,
    v_hbm,
    lists,
    counts,
    w_hbm,
    out,
    q_all,
    t_all,
    t_wide,
    hot,
    k_all,
    v_all,
    v_stage,
    top_now,
    sum_now,
    acc,
    o_own,
    o_out,
    o_in,
    st_out,
    st_in,
    a_out,
    a_all,
    w_all,
    part,
    r_out,
    r_in,
    load_sem,
    kv_send,
    kv_recv,
    q_send,
    q_recv,
    t_send,
    t_recv,
    o_send,
    o_recv,
    st_send,
    st_recv,
    a_send,
    a_recv,
    w_send,
    w_recv,
    r_send,
    r_recv,
):
    nx, ny, nz, nd = sizes
    heads, rows = q_hbm.shape[2] // HD, q_hbm.shape[1]
    take = rows // (2 * nz)
    far = ny // 2
    u, b, d = lax.axis_index("uly"), lax.axis_index("blk"), lax.axis_index("dp")
    z, core = u // 2, u % 2
    y, x = b // nx, b % nx

    def at_y(step):
        return {"blk": lax.rem(y + step + ny, ny) * nx + x}

    def at_x(step):
        return {"blk": y * nx + lax.rem(x + step + nx, nx)}

    def at_z(step):
        return {"uly": lax.rem(z + step + nz, nz) * 2 + core}

    def at_a(flip, step):
        return {
            "uly": z * 2 + lax.rem(core + flip, 2),
            "dp": lax.rem(d + step + nd, nd),
        }

    def send(src, dst, send_sem, recv_sem, device):
        return pltpu.make_async_remote_copy(
            src_ref=src,
            dst_ref=dst,
            send_sem=send_sem,
            recv_sem=recv_sem,
            device_id=device,
            device_id_type=MESH,
        )

    def kv_copy(h, way, step, which):
        buffer = (k_all, v_all)[which]
        old, new = (step - 1, step) if way == 0 else ((ny - step + 1) % ny, ny - step)
        return send(
            buffer.at[h, old],
            buffer.at[h, new],
            kv_send.at[h, way, step - 1, which],
            kv_recv.at[h, new, which],
            at_y(1 - 2 * way),
        )

    def q_copy(h, j):
        return send(
            q_all.at[h, 0], q_all.at[h, j], q_send.at[h, j], q_recv.at[h, j], at_x(j)
        )

    def t_copy(j):
        return send(t_all.at[0], t_all.at[j], t_send.at[j], t_recv.at[j], at_x(j))

    def o_copy(h, j):
        return send(
            o_out.at[h, j], o_in.at[h, j], o_send.at[h, j], o_recv.at[h, j], at_x(-j)
        )

    def st_copy(h, j):
        return send(
            st_out.at[h, j],
            st_in.at[h, j],
            st_send.at[h, j],
            st_recv.at[h, j],
            at_x(-j),
        )

    def a_copy(h, flip, step):
        return send(
            a_out.at[h, lax.rem(core + flip, 2)],
            a_all.at[h, step, :, pl.ds(flip * HD, HD)],
            a_send.at[h, flip, step],
            a_recv.at[h, flip, step],
            at_a(flip, step),
        )

    def a_relay(h, flip):
        old = 1 if flip == 0 else nd - 1
        lanes = pl.ds(flip * HD, HD)
        return send(
            a_all.at[h, old, :, lanes],
            a_all.at[h, 2, :, lanes],
            a_send.at[h, flip, 2],
            a_recv.at[h, flip, 2],
            at_a(0, 1 if flip == 0 else -1),
        )

    def w_copy(h):
        return send(
            w_hbm.at[pl.ds(h * HD, HD), :],
            w_all.at[h, pl.ds(HD, HD), :],
            w_send.at[h],
            w_recv.at[h],
            at_a(1, 0),
        )

    def r_copy(j, step):
        return send(
            r_out.at[j, step],
            r_in.at[j, step],
            r_send.at[j, step],
            r_recv.at[j, step],
            at_z(j),
        )

    started = []

    def start(copy):
        copy.start()
        started.append(copy)

    def ways(step):
        pairs = []
        for which in range(2):
            for way in range(2):
                if step < far or which == way:
                    pairs.append((way, which))
        return pairs

    def load(src, dst, sem):
        copy = pltpu.make_async_copy(src, dst, sem)
        copy.start()
        return copy

    load_k = [
        load(k_hbm.at[0, :, pl.ds(h * HD, HD)], k_all.at[h, 0], load_sem.at[0, h])
        for h in range(heads)
    ]
    load_v = [
        load(v_hbm.at[0, :, pl.ds(h * HD, HD)], v_stage.at[h], load_sem.at[1, h])
        for h in range(heads)
    ]
    load_q = [
        load(q_hbm.at[0, :, pl.ds(h * HD, HD)], q_all.at[h, 0], load_sem.at[2, h])
        for h in range(heads)
    ]
    load_w = [
        load(
            w_hbm.at[pl.ds(h * HD, HD), :],
            w_all.at[h, pl.ds(0, HD), :],
            load_sem.at[3, h],
        )
        for h in range(heads)
    ]

    barrier = pltpu.get_barrier_semaphore()
    around = [at_y(1), at_y(-1)]
    around += [at_x(j) for j in range(1, nx)]
    near = sorted({1 % nd, nd - 1} - {0})
    around += [at_a(f, s) for s in [0] + near for f in range(2) if f or s]
    around += [at_z(j) for j in range(1, nz)]
    for device in around:
        pl.semaphore_signal(barrier, inc=1, device_id=device, device_id_type=MESH)

    lane = lax.broadcasted_iota(jnp.int32, (1, HD), 1)
    for h in range(heads):
        for i in range(rows // BLOCK):
            seen = jnp.zeros((1, HD), jnp.int32)
            live = counts[0, i, h]
            for n in range(lists.shape[3]):
                hit = (lane == lists[0, h, i, n]) & (jnp.full((1, HD), n) < live)
                seen = seen | hit.astype(jnp.int32)
            line = h * (rows // BLOCK) + i
            t_all[0, line : line + 1, :] = jnp.where(seen > 0, 0.0, MASKED)

    for copy in load_k:
        copy.wait()
    load_v[0].wait()
    v_all[0, 0] = v_stage[0].T
    load_q[0].wait()
    pl.semaphore_wait(barrier, len(around))

    for way, which in ways(1):
        start(kv_copy(0, way, 1, which))
    load_v[1].wait()
    v_all[1, 0] = v_stage[1].T
    for way, which in ways(1):
        start(kv_copy(1, way, 1, which))
    for j in range(1, nx):
        start(t_copy(j))
        start(q_copy(0, j))

    row = lax.broadcasted_iota(jnp.int32, (rows, HD), 0)
    column = lax.broadcasted_iota(jnp.int32, (rows, HD), 1)
    per = rows // BLOCK
    for s in range(ny):
        owner = lax.rem(y - s + ny, ny) * nx + x
        hot[s] = jnp.where(column == owner * per + row // BLOCK, 1.0, 0.0).astype(BF16)

    for h in range(1, heads):
        if h > 1:
            load_v[h].wait()
            v_all[h, 0] = v_stage[h].T
        load_q[h].wait()
        for j in range(1, nx):
            start(q_copy(h, j))
    for h in range(heads):
        start(w_copy(h))

    for j in range(1, nx):
        t_copy(j).wait_recv()
    for h in range(heads):
        for j in range(nx):
            for i in range(per):
                line = h * per + i
                wide = jnp.broadcast_to(t_all[j, line : line + 1, :], (BLOCK, HD))
                t_wide[h, j, i * BLOCK : (i + 1) * BLOCK, :] = wide.astype(BF16)

    def attend(h, slots, first):
        keys = jnp.concatenate(
            [jnp.concatenate([k_all[h, s], hot[s]], axis=1) for s in slots], axis=0
        )
        values = jnp.concatenate([v_all[h, s] for s in slots], axis=1)
        queries = jnp.concatenate(
            [q_all[h].reshape(nx * rows, HD), t_wide[h].reshape(nx * rows, HD)], axis=1
        )
        scores = lax.dot_general(
            keys, queries, (((1,), (1,)), ((), ())), preferred_element_type=F32
        )
        top = jnp.max(scores, axis=0, keepdims=True)
        if not first:
            old = top_now[h]
            top = jnp.maximum(top, old)
        probs = jnp.exp2((scores - top) * SCALE)
        total = jnp.sum(probs, axis=0, keepdims=True)
        mixed = jnp.dot(values, probs.astype(BF16), preferred_element_type=F32)
        if not first:
            fade = jnp.exp2((old - top) * SCALE)
            total = total + sum_now[h] * fade
            mixed = mixed + acc[h] * fade
        top_now[h] = top
        sum_now[h] = total
        acc[h] = mixed

    def share(h):
        for j in range(nx):
            lanes = slice(j * rows, (j + 1) * rows)
            st_out[h, j, 0:1, :] = top_now[h, :, lanes]
            st_out[h, j, 1:2, :] = sum_now[h, :, lanes]
            if j == 0:
                o_own[h] = acc[h, :, lanes]
            else:
                o_out[h, j] = acc[h, :, lanes].astype(BF16)
                start(st_copy(h, j))
                start(o_copy(h, j))

    def merge(h):
        for j in range(1, nx):
            st_copy(h, j).wait_recv()
        tops = [st_out[h, 0, 0:1, :]] + [st_in[h, j, 0:1, :] for j in range(1, nx)]
        sums = [st_out[h, 0, 1:2, :]] + [st_in[h, j, 1:2, :] for j in range(1, nx)]
        top = functools.reduce(jnp.maximum, tops)
        weights = [jnp.exp2((t - top) * SCALE) for t in tops]
        denom = sum(w * s for w, s in zip(weights, sums))
        total = o_own[h] * weights[0]
        for j in range(1, nx):
            o_copy(h, j).wait_recv()
            total = total + o_in[h, j].astype(F32) * weights[j]
        attended = (total / denom).T.astype(BF16)
        for i in range(2 * nz):
            place = slice(i // 2 * take, (i // 2 + 1) * take)
            a_out[h, i % 2, place, :] = attended[i * take : (i + 1) * take, :]
        for step in near + [0]:
            for flip in range(2):
                if flip or step:
                    start(a_copy(h, flip, step))
        a_all[h, 0, :, 0:HD] = a_out[h, core]

    arrived = set()

    def receive(h, flip, step):
        if (flip or step) and (h, flip, step) not in arrived:
            arrived.add((h, flip, step))
            a_copy(h, flip, step).wait_recv()

    def relay(h):
        if nd > 3:
            for flip in range(2):
                receive(h, flip, 1 if flip == 0 else nd - 1)
                start(a_relay(h, flip))

    def receive_keys(h, step):
        for way, which in ways(step):
            kv_copy(h, way, step, which).wait_recv()
            if step < far and (way, which) in ways(step + 1):
                start(kv_copy(h, way, step + 1, which))

    last = heads - 1
    events = sorted((h + step, -h, step) for h in range(heads) for step in range(1, far + 1))
    for _, h, step in events:
        h = -h
        receive_keys(h, step)
        if step == 1:
            if h + 2 < heads:
                for way, which in ways(1):
                    start(kv_copy(h + 2, way, 1, which))
            for j in range(1, nx):
                q_copy(h, j).wait_recv()
        slots = [0] * (step == 1) + ([step, ny - step] if step < far else [far])
        attend(h, slots, step == 1)
        if step == far:
            share(h)
        if (h, step) == (last, far - 1):
            merge(0)
    for h in range(1, heads):
        merge(h)
    for h in range(heads):
        relay(h)
    for h in range(heads):
        load_w[h].wait()
        w_copy(h).wait_recv()

    lines, depth = nz * take, heads * 2 * HD
    weights = w_all[...].reshape(depth, w_all.shape[2])
    for step in [0] + near + list(range(2, nd - 1)):
        for h in range(heads):
            for flip in range(2):
                receive(h, flip, step)
        rows_in = jnp.concatenate([a_all[h, step] for h in range(heads)], axis=1)
        mixed = jnp.dot(rows_in, weights, preferred_element_type=F32)
        part[step] = mixed.reshape(nz, take, mixed.shape[1])
        for j in range(1, nz):
            goal = lax.rem(z + j, nz)
            r_out[j, step] = part[step, goal].astype(BF16)
            start(r_copy(j, step))
    for step in range(nd):
        total = part[step, z]
        for j in range(1, nz):
            r_copy(j, step).wait_recv()
            total = total + r_in[j, step].astype(F32)
        out[lax.rem(d - step + nd, nd)] = total.astype(BF16)

    for copy in started:
        copy.wait_send()


def on_device(sizes, queries, keys, values, block_lists, block_counts, w_out):
    nx, ny, nz, nd = sizes
    rows, heads = queries.shape[1], queries.shape[2] // HD
    take, width = rows // (2 * nz), w_out.shape[1]
    dma = pltpu.SemaphoreType.DMA
    far = ny // 2
    return pl.pallas_call(
        functools.partial(fused, sizes),
        out_shape=jax.ShapeDtypeStruct((nd, take, width), BF16),
        in_specs=[pl.BlockSpec(memory_space=pl.ANY)] * 3
        + [pl.BlockSpec(memory_space=pltpu.SMEM)] * 2
        + [pl.BlockSpec(memory_space=pl.ANY)],
        out_specs=pl.BlockSpec(memory_space=pltpu.VMEM),
        scratch_shapes=[
            pltpu.VMEM((heads, nx, rows, HD), BF16),
            pltpu.VMEM((nx, 8, HD), F32),
            pltpu.VMEM((heads, nx, rows, HD), BF16),
            pltpu.VMEM((ny, rows, HD), BF16),
            pltpu.VMEM((heads, ny, rows, HD), BF16),
            pltpu.VMEM((heads, ny, HD, rows), BF16),
            pltpu.VMEM((heads, rows, HD), BF16),
            pltpu.VMEM((heads, 1, nx * rows), F32),
            pltpu.VMEM((heads, 1, nx * rows), F32),
            pltpu.VMEM((heads, HD, nx * rows), F32),
            pltpu.VMEM((heads, HD, rows), F32),
            pltpu.VMEM((heads, nx, HD, rows), BF16),
            pltpu.VMEM((heads, nx, HD, rows), BF16),
            pltpu.VMEM((heads, nx, 8, rows), F32),
            pltpu.VMEM((heads, nx, 8, rows), F32),
            pltpu.VMEM((heads, 2, nz * take, HD), BF16),
            pltpu.VMEM((heads, nd, nz * take, 2 * HD), BF16),
            pltpu.VMEM((heads, 2 * HD, width), BF16),
            pltpu.VMEM((nd, nz, take, width), F32),
            pltpu.VMEM((nz, nd, take, width), BF16),
            pltpu.VMEM((nz, nd, take, width), BF16),
            dma((4, heads)),
            dma((heads, 2, far, 2)),
            dma((heads, ny, 2)),
            dma((heads, nx)),
            dma((heads, nx)),
            dma((nx,)),
            dma((nx,)),
            dma((heads, nx)),
            dma((heads, nx)),
            dma((heads, nx)),
            dma((heads, nx)),
            dma((heads, 2, nd)),
            dma((heads, 2, nd)),
            dma((heads,)),
            dma((heads,)),
            dma((nz, nd)),
            dma((nz, nd)),
        ],
        compiler_params=pltpu.CompilerParams(
            collective_id=0, has_side_effects=True, vmem_limit_bytes=60 * 2**20
        ),
        name="attention",
    )(queries, keys, values, block_lists, block_counts.transpose(0, 2, 1), w_out)


def solution(mesh):
    shape = mesh.shape
    sizes = (X_SIZE, shape["blk"] // X_SIZE, shape["uly"] // 2, shape["dp"])
    placed = (
        P("dp", "blk", "uly"),
        P("dp", "blk", "uly"),
        P("dp", "blk", "uly"),
        P("dp", "uly", "blk", None),
        P("dp", "uly", "blk"),
        P("uly", "dp"),
    )
    return jax.shard_map(
        functools.partial(on_device, sizes),
        mesh=mesh,
        in_specs=placed,
        out_specs=P(None, ("blk", "uly"), "dp"),
        check_vma=False,
    )
```

```python
import functools
import math

import jax
import jax.numpy as jnp
from jax import lax
from jax.experimental import pallas as pl
from jax.experimental.pallas import tpu as pltpu
from jax.sharding import PartitionSpec as P

HD = 128
BLOCK = 64
X_SIZE = 4
MASKED = -1e30
SCALE = HD**-0.5 * math.log2(math.e)
MESH = pl.DeviceIdType.MESH
F32 = jnp.float32
BF16 = jnp.bfloat16


def fused(
    sizes,
    q_hbm,
    k_hbm,
    v_hbm,
    lists,
    counts,
    w_hbm,
    out,
    q_all,
    t_all,
    t_wide,
    hot,
    kv_all,
    v_stage,
    top_now,
    sum_now,
    acc,
    o_own,
    o_out,
    o_in,
    st_out,
    st_in,
    a_out,
    a_all,
    w_all,
    part,
    r_out,
    r_in,
    load_sem,
    kv_send,
    kv_recv,
    q_send,
    q_recv,
    t_send,
    t_recv,
    o_send,
    o_recv,
    st_send,
    st_recv,
    a_send,
    a_recv,
    w_send,
    w_recv,
    r_send,
    r_recv,
    word,
):
    nx, ny, nz, nd = sizes
    heads, rows = q_hbm.shape[2] // HD, q_hbm.shape[1]
    take = rows // (2 * nz)
    far = ny // 2
    u, b, d = lax.axis_index("uly"), lax.axis_index("blk"), lax.axis_index("dp")
    z, core = u // 2, u % 2
    y, x = b // nx, b % nx

    def at_y(step):
        return {"blk": lax.rem(y + step + ny, ny) * nx + x}

    def at_x(step):
        return {"blk": y * nx + lax.rem(x + step + nx, nx)}

    def at_z(step):
        return {"uly": lax.rem(z + step + nz, nz) * 2 + core}

    def at_ring(step):
        place = lax.rem(d * nz + z + step + nd * nz, nd * nz)
        return {"uly": lax.rem(place, nz) * 2 + core, "dp": place // nz}

    def pass_word(turn):
        if turn:
            pl.semaphore_wait(word.at[turn - 1, 0], 1)
            pl.semaphore_wait(word.at[turn - 1, 1], 1)
        if turn < nz:
            for way, device in enumerate(beside):
                pl.semaphore_signal(
                    word.at[turn, way], inc=1, device_id=device, device_id_type=MESH
                )

    def at_a(flip, step):
        return {
            "uly": z * 2 + lax.rem(core + flip, 2),
            "dp": lax.rem(d + step + nd, nd),
        }

    def send(src, dst, send_sem, recv_sem, device):
        return pltpu.make_async_remote_copy(
            src_ref=src,
            dst_ref=dst,
            send_sem=send_sem,
            recv_sem=recv_sem,
            device_id=device,
            device_id_type=MESH,
        )

    def kv_copy(h, way, step):
        old, new = (step - 1, step) if way == 0 else ((ny - step + 1) % ny, ny - step)
        src, dst = kv_all.at[h, old], kv_all.at[h, new]
        if step == far:
            src, dst = kv_all.at[h, old, way], kv_all.at[h, new, way]
        return send(
            src,
            dst,
            kv_send.at[h, way, step - 1],
            kv_recv.at[h, new if (way, step) != (1, far) else ny],
            at_y(1 - 2 * way),
        )

    def q_copy(h, j):
        return send(
            q_all.at[h, 0], q_all.at[h, j], q_send.at[h, j], q_recv.at[h, j], at_x(j)
        )

    def t_copy(j):
        return send(t_all.at[0], t_all.at[j], t_send.at[j], t_recv.at[j], at_x(j))

    def o_copy(h, j):
        return send(
            o_out.at[h, j], o_in.at[h, j], o_send.at[h, j], o_recv.at[h, j], at_x(-j)
        )

    def st_copy(h, j):
        return send(
            st_out.at[h, j],
            st_in.at[h, j],
            st_send.at[h, j],
            st_recv.at[h, j],
            at_x(-j),
        )

    def a_copy(h, flip, step):
        return send(
            a_out.at[h, lax.rem(core + flip, 2)],
            a_all.at[h, step, :, pl.ds(flip * HD, HD)],
            a_send.at[h, flip, step],
            a_recv.at[h, flip, step],
            at_a(flip, step),
        )

    def a_relay(h, flip):
        old = 1 if flip == 0 else nd - 1
        lanes = pl.ds(flip * HD, HD)
        return send(
            a_all.at[h, old, :, lanes],
            a_all.at[h, 2, :, lanes],
            a_send.at[h, flip, 2],
            a_recv.at[h, flip, 2],
            at_a(0, 1 if flip == 0 else -1),
        )

    def w_copy(h):
        return send(
            w_hbm.at[pl.ds(h * HD, HD), :],
            w_all.at[h, pl.ds(HD, HD), :],
            w_send.at[h],
            w_recv.at[h],
            at_a(1, 0),
        )

    def r_copy(j, step):
        return send(
            r_out.at[j, step],
            r_in.at[j, step],
            r_send.at[j, step],
            r_recv.at[j, step],
            at_z(j),
        )

    started = []

    def start(copy):
        copy.start()
        started.append(copy)

    def load(src, dst, sem):
        copy = pltpu.make_async_copy(src, dst, sem)
        copy.start()
        return copy

    load_k = [
        load(k_hbm.at[0, :, pl.ds(h * HD, HD)], kv_all.at[h, 0, 0], load_sem.at[0, h])
        for h in range(heads)
    ]
    load_v = [
        load(v_hbm.at[0, :, pl.ds(h * HD, HD)], v_stage.at[h], load_sem.at[1, h])
        for h in range(heads)
    ]
    load_q = [
        load(q_hbm.at[0, :, pl.ds(h * HD, HD)], q_all.at[h, 0], load_sem.at[2, h])
        for h in range(heads)
    ]
    load_w = [
        load(
            w_hbm.at[pl.ds(h * HD, HD), :],
            w_all.at[h, pl.ds(0, HD), :],
            load_sem.at[3, h],
        )
        for h in range(heads)
    ]

    beside = [at_ring(1), at_ring(-1)] if nz * nd > 1 else []
    barrier = pltpu.get_barrier_semaphore()
    around = [at_y(1), at_y(-1)]
    around += [at_x(j) for j in range(1, nx)]
    near = sorted({1 % nd, nd - 1} - {0})
    around += [at_a(1, 0)]
    around += beside
    for device in around:
        pl.semaphore_signal(barrier, inc=1, device_id=device, device_id_type=MESH)

    lane = lax.broadcasted_iota(jnp.int32, (1, HD), 1)
    for h in range(heads):
        for i in range(rows // BLOCK):
            seen = jnp.zeros((1, HD), jnp.int32)
            live = counts[0, i, h]
            for n in range(lists.shape[3]):
                hit = (lane == lists[0, h, i, n]) & (jnp.full((1, HD), n) < live)
                seen = seen | hit.astype(jnp.int32)
            line = h * (rows // BLOCK) + i
            t_all[0, line : line + 1, :] = jnp.where(seen > 0, 0.0, MASKED)

    for copy in load_k:
        copy.wait()
    load_v[0].wait()
    kv_all[0, 0, 1] = v_stage[0].T
    load_q[0].wait()
    pl.semaphore_wait(barrier, len(around))

    for way in range(2):
        start(kv_copy(0, way, 1))
    for j in range(1, nx):
        start(t_copy(j))
        start(q_copy(0, j))

    for h in range(1, heads):
        load_v[h].wait()
        kv_all[h, 0, 1] = v_stage[h].T
        for way in range(2):
            start(kv_copy(h, way, 1))
    for h in range(1, heads):
        load_q[h].wait()
        for j in range(1, nx):
            start(q_copy(h, j))
    for h in range(heads):
        start(w_copy(h))

    row = lax.broadcasted_iota(jnp.int32, (rows, HD), 0)
    column = lax.broadcasted_iota(jnp.int32, (rows, HD), 1)
    per = rows // BLOCK
    for s in range(ny):
        owner = lax.rem(y - s + ny, ny) * nx + x
        hot[s] = jnp.where(column == owner * per + row // BLOCK, 1.0, 0.0).astype(BF16)

    for j in range(1, nx):
        t_copy(j).wait_recv()
    for h in range(heads):
        for j in range(nx):
            for i in range(per):
                line = h * per + i
                wide = jnp.broadcast_to(t_all[j, line : line + 1, :], (BLOCK, HD))
                t_wide[h, j, i * BLOCK : (i + 1) * BLOCK, :] = wide.astype(BF16)

    def attend(h, slots, first):
        keys = jnp.concatenate(
            [jnp.concatenate([kv_all[h, s, 0], hot[s]], axis=1) for s in slots], axis=0
        )
        values = jnp.concatenate([kv_all[h, s, 1] for s in slots], axis=1)
        queries = jnp.concatenate(
            [q_all[h].reshape(nx * rows, HD), t_wide[h].reshape(nx * rows, HD)], axis=1
        )
        scores = lax.dot_general(
            keys, queries, (((1,), (1,)), ((), ())), preferred_element_type=F32
        )
        top = jnp.max(scores, axis=0, keepdims=True)
        if not first:
            old = top_now[h]
            top = jnp.maximum(top, old)
        probs = jnp.exp2((scores - top) * SCALE)
        total = jnp.sum(probs, axis=0, keepdims=True)
        mixed = jnp.dot(values, probs.astype(BF16), preferred_element_type=F32)
        if not first:
            fade = jnp.exp2((old - top) * SCALE)
            total = total + sum_now[h] * fade
            mixed = mixed + acc[h] * fade
        top_now[h] = top
        sum_now[h] = total
        acc[h] = mixed

    def share(h):
        for j in range(nx):
            lanes = slice(j * rows, (j + 1) * rows)
            st_out[h, j, 0:1, :] = top_now[h, :, lanes]
            st_out[h, j, 1:2, :] = sum_now[h, :, lanes]
            if j == 0:
                o_own[h] = acc[h, :, lanes]
            else:
                o_out[h, j] = acc[h, :, lanes].astype(BF16)
                start(st_copy(h, j))
                start(o_copy(h, j))

    def merge(h):
        for j in range(1, nx):
            st_copy(h, j).wait_recv()
        tops = [st_out[h, 0, 0:1, :]] + [st_in[h, j, 0:1, :] for j in range(1, nx)]
        sums = [st_out[h, 0, 1:2, :]] + [st_in[h, j, 1:2, :] for j in range(1, nx)]
        top = functools.reduce(jnp.maximum, tops)
        weights = [jnp.exp2((t - top) * SCALE) for t in tops]
        denom = sum(w * s for w, s in zip(weights, sums))
        total = o_own[h] * weights[0]
        for j in range(1, nx):
            o_copy(h, j).wait_recv()
            total = total + o_in[h, j].astype(F32) * weights[j]
        attended = (total / denom).T.astype(BF16)
        for i in range(2 * nz):
            place = slice(i // 2 * take, (i // 2 + 1) * take)
            a_out[h, i % 2, place, :] = attended[i * take : (i + 1) * take, :]
        for step in near + [0]:
            for flip in range(2):
                if flip or step:
                    start(a_copy(h, flip, step))
        a_all[h, 0, :, 0:HD] = a_out[h, core]

    arrived = set()

    def receive(h, flip, step):
        if (flip or step) and (h, flip, step) not in arrived:
            arrived.add((h, flip, step))
            a_copy(h, flip, step).wait_recv()

    def relay(h):
        if nd > 3:
            for flip in range(2):
                receive(h, flip, 1 if flip == 0 else nd - 1)
                start(a_relay(h, flip))

    def receive_keys(h, step):
        for way in range(2):
            kv_copy(h, way, step).wait_recv()
            if step < far:
                start(kv_copy(h, way, step + 1))

    last = heads - 1
    events = [(h, step) for step in range(1, far + 1) for h in range(heads)]
    for n, (h, step) in enumerate(events):
        receive_keys(h, step)
        if beside and n % 2 == 0 and n // 2 <= nz:
            pass_word(n // 2)
        if step == 1:
            for j in range(1, nx):
                q_copy(h, j).wait_recv()
        slots = [0] * (step == 1) + ([step, ny - step] if step < far else [far])
        attend(h, slots, step == 1)
        if step == far:
            share(h)
    for h in range(heads):
        merge(h)
    relay(0)
    for h in range(heads):
        load_w[h].wait()
        w_copy(h).wait_recv()

    lines, depth = nz * take, heads * 2 * HD
    weights = w_all[...].reshape(depth, w_all.shape[2])
    for step in [0] + near + list(range(2, nd - 1)):
        if near and step == near[0]:
            for h in range(1, heads):
                relay(h)
        for h in range(heads):
            for flip in range(2):
                receive(h, flip, step)
        rows_in = jnp.concatenate([a_all[h, step] for h in range(heads)], axis=1)
        mixed = jnp.dot(rows_in, weights, preferred_element_type=F32)
        part[step] = mixed.reshape(nz, take, mixed.shape[1])
        for j in range(1, nz):
            goal = lax.rem(z + j, nz)
            r_out[j, step] = part[step, goal].astype(BF16)
            start(r_copy(j, step))
    for step in range(nd):
        total = part[step, z]
        for j in range(1, nz):
            r_copy(j, step).wait_recv()
            total = total + r_in[j, step].astype(F32)
        out[lax.rem(d - step + nd, nd)] = total.astype(BF16)

    for copy in started:
        copy.wait_send()


def on_device(sizes, queries, keys, values, block_lists, block_counts, w_out):
    nx, ny, nz, nd = sizes
    rows, heads = queries.shape[1], queries.shape[2] // HD
    take, width = rows // (2 * nz), w_out.shape[1]
    dma = pltpu.SemaphoreType.DMA
    far = ny // 2
    return pl.pallas_call(
        functools.partial(fused, sizes),
        out_shape=jax.ShapeDtypeStruct((nd, take, width), BF16),
        in_specs=[pl.BlockSpec(memory_space=pl.ANY)] * 3
        + [pl.BlockSpec(memory_space=pltpu.SMEM)] * 2
        + [pl.BlockSpec(memory_space=pl.ANY)],
        out_specs=pl.BlockSpec(memory_space=pltpu.VMEM),
        scratch_shapes=[
            pltpu.VMEM((heads, nx, rows, HD), BF16),
            pltpu.VMEM((nx, 8, HD), F32),
            pltpu.VMEM((heads, nx, rows, HD), BF16),
            pltpu.VMEM((ny, rows, HD), BF16),
            pltpu.VMEM((heads, ny, 2, rows, HD), BF16),
            pltpu.VMEM((heads, rows, HD), BF16),
            pltpu.VMEM((heads, 1, nx * rows), F32),
            pltpu.VMEM((heads, 1, nx * rows), F32),
            pltpu.VMEM((heads, HD, nx * rows), F32),
            pltpu.VMEM((heads, HD, rows), F32),
            pltpu.VMEM((heads, nx, HD, rows), BF16),
            pltpu.VMEM((heads, nx, HD, rows), BF16),
            pltpu.VMEM((heads, nx, 8, rows), F32),
            pltpu.VMEM((heads, nx, 8, rows), F32),
            pltpu.VMEM((heads, 2, nz * take, HD), BF16),
            pltpu.VMEM((heads, nd, nz * take, 2 * HD), BF16),
            pltpu.VMEM((heads, 2 * HD, width), BF16),
            pltpu.VMEM((nd, nz, take, width), F32),
            pltpu.VMEM((nz, nd, take, width), BF16),
            pltpu.VMEM((nz, nd, take, width), BF16),
            dma((4, heads)),
            dma((heads, 2, far)),
            dma((heads, ny + 1)),
            dma((heads, nx)),
            dma((heads, nx)),
            dma((nx,)),
            dma((nx,)),
            dma((heads, nx)),
            dma((heads, nx)),
            dma((heads, nx)),
            dma((heads, nx)),
            dma((heads, 2, nd)),
            dma((heads, 2, nd)),
            dma((heads,)),
            dma((heads,)),
            dma((nz, nd)),
            dma((nz, nd)),
            pltpu.SemaphoreType.REGULAR((nz, 2)),
        ],
        compiler_params=pltpu.CompilerParams(
            collective_id=0, has_side_effects=True, vmem_limit_bytes=60 * 2**20
        ),
        name="attention",
    )(queries, keys, values, block_lists, block_counts.transpose(0, 2, 1), w_out)


def solution(mesh):
    shape = mesh.shape
    sizes = (X_SIZE, shape["blk"] // X_SIZE, shape["uly"] // 2, shape["dp"])
    placed = (
        P("dp", "blk", "uly"),
        P("dp", "blk", "uly"),
        P("dp", "blk", "uly"),
        P("dp", "uly", "blk", None),
        P("dp", "uly", "blk"),
        P("uly", "dp"),
    )
    return jax.shard_map(
        functools.partial(on_device, sizes),
        mesh=mesh,
        in_specs=placed,
        out_specs=P(None, ("blk", "uly"), "dp"),
        check_vma=False,
    )
```

```python
import functools
import math

import jax
import jax.numpy as jnp
from jax import lax
from jax.experimental import pallas as pl
from jax.experimental.pallas import tpu as pltpu
from jax.sharding import PartitionSpec as P

HD = 128
BLOCK = 64
X_SIZE = 4
MASKED = -1e30
SCALE = HD**-0.5 * math.log2(math.e)
MESH = pl.DeviceIdType.MESH
F32 = jnp.float32
BF16 = jnp.bfloat16


def fused(
    sizes,
    q_hbm,
    k_hbm,
    v_hbm,
    lists,
    counts,
    w_hbm,
    out,
    q_all,
    t_all,
    t_wide,
    hot,
    kv_all,
    v_stage,
    top_now,
    sum_now,
    acc,
    o_own,
    o_out,
    o_in,
    st_out,
    a_out,
    a_all,
    w_all,
    part,
    r_out,
    r_in,
    load_sem,
    kv_send,
    kv_recv,
    q_send,
    q_recv,
    t_send,
    t_recv,
    o_send,
    o_recv,
    a_send,
    a_recv,
    w_send,
    w_recv,
    r_send,
    r_recv,
    word,
):
    nx, ny, nz, nd = sizes
    heads, rows = q_hbm.shape[2] // HD, q_hbm.shape[1]
    take = rows // (2 * nz)
    far = ny // 2
    u, b, d = lax.axis_index("uly"), lax.axis_index("blk"), lax.axis_index("dp")
    z, core = u // 2, u % 2
    y, x = b // nx, b % nx

    def at_y(step):
        return {"blk": lax.rem(y + step + ny, ny) * nx + x}

    def at_x(step):
        return {"blk": y * nx + lax.rem(x + step + nx, nx)}

    def at_z(step):
        return {"uly": lax.rem(z + step + nz, nz) * 2 + core}

    def at_ring(step):
        place = lax.rem(d * nz + z + step + nd * nz, nd * nz)
        return {"uly": lax.rem(place, nz) * 2 + core, "dp": place // nz}

    def pass_word(turn):
        if turn:
            pl.semaphore_wait(word.at[turn - 1, 0], 1)
            pl.semaphore_wait(word.at[turn - 1, 1], 1)
        if turn < nz:
            for way, device in enumerate(beside):
                pl.semaphore_signal(
                    word.at[turn, way], inc=1, device_id=device, device_id_type=MESH
                )

    def at_a(flip, step):
        return {
            "uly": z * 2 + lax.rem(core + flip, 2),
            "dp": lax.rem(d + step + nd, nd),
        }

    def send(src, dst, send_sem, recv_sem, device):
        return pltpu.make_async_remote_copy(
            src_ref=src,
            dst_ref=dst,
            send_sem=send_sem,
            recv_sem=recv_sem,
            device_id=device,
            device_id_type=MESH,
        )

    def kv_copy(h, way, step):
        old, new = (step - 1, step) if way == 0 else ((ny - step + 1) % ny, ny - step)
        src, dst = kv_all.at[h, old], kv_all.at[h, new]
        if step == far:
            src, dst = kv_all.at[h, old, way], kv_all.at[h, new, way]
        return send(
            src,
            dst,
            kv_send.at[h, way, step - 1],
            kv_recv.at[h, new if (way, step) != (1, far) else ny],
            at_y(1 - 2 * way),
        )

    def q_copy(h, j):
        return send(
            q_all.at[h, 0], q_all.at[h, j], q_send.at[h, j], q_recv.at[h, j], at_x(j)
        )

    def t_copy(j):
        return send(t_all.at[0], t_all.at[j], t_send.at[j], t_recv.at[j], at_x(j))

    def o_copy(h, j):
        return send(
            o_out.at[h, j], o_in.at[h, j], o_send.at[h, j], o_recv.at[h, j], at_x(-j)
        )

    def a_copy(h, flip, step):
        return send(
            a_out.at[h, lax.rem(core + flip, 2)],
            a_all.at[h, step, :, pl.ds(flip * HD, HD)],
            a_send.at[h, flip, step],
            a_recv.at[h, flip, step],
            at_a(flip, step),
        )

    def a_relay(h, flip):
        old = 1 if flip == 0 else nd - 1
        lanes = pl.ds(flip * HD, HD)
        return send(
            a_all.at[h, old, :, lanes],
            a_all.at[h, 2, :, lanes],
            a_send.at[h, flip, 2],
            a_recv.at[h, flip, 2],
            at_a(0, 1 if flip == 0 else -1),
        )

    def w_copy(h):
        return send(
            w_hbm.at[pl.ds(h * HD, HD), :],
            w_all.at[h, pl.ds(HD, HD), :],
            w_send.at[h],
            w_recv.at[h],
            at_a(1, 0),
        )

    def r_copy(j, step):
        return send(
            r_out.at[j, step],
            r_in.at[j, step],
            r_send.at[j, step],
            r_recv.at[j, step],
            at_z(j),
        )

    started = []

    def start(copy):
        copy.start()
        started.append(copy)

    def load(src, dst, sem):
        copy = pltpu.make_async_copy(src, dst, sem)
        copy.start()
        return copy

    load_k = [
        load(k_hbm.at[0, :, pl.ds(h * HD, HD)], kv_all.at[h, 0, 0], load_sem.at[0, h])
        for h in range(heads)
    ]
    load_v = [
        load(v_hbm.at[0, :, pl.ds(h * HD, HD)], v_stage.at[h], load_sem.at[1, h])
        for h in range(heads)
    ]
    load_q = [
        load(q_hbm.at[0, :, pl.ds(h * HD, HD)], q_all.at[h, 0], load_sem.at[2, h])
        for h in range(heads)
    ]
    load_w = [
        load(
            w_hbm.at[pl.ds(h * HD, HD), :],
            w_all.at[h, pl.ds(0, HD), :],
            load_sem.at[3, h],
        )
        for h in range(heads)
    ]

    beside = [at_ring(1), at_ring(-1)] if nz * nd > 1 else []
    barrier = pltpu.get_barrier_semaphore()
    around = [at_y(1), at_y(-1)]
    around += [at_x(j) for j in range(1, nx)]
    near = sorted({1 % nd, nd - 1} - {0})
    around += [at_a(1, 0)]
    around += beside
    for device in around:
        pl.semaphore_signal(barrier, inc=1, device_id=device, device_id_type=MESH)

    lane = lax.broadcasted_iota(jnp.int32, (1, HD), 1)
    for h in range(heads):
        for i in range(rows // BLOCK):
            seen = jnp.zeros((1, HD), jnp.int32)
            live = counts[0, i, h]
            for n in range(lists.shape[3]):
                hit = (lane == lists[0, h, i, n]) & (jnp.full((1, HD), n) < live)
                seen = seen | hit.astype(jnp.int32)
            line = h * (rows // BLOCK) + i
            t_all[0, line : line + 1, :] = jnp.where(seen > 0, 0.0, MASKED)

    for copy in load_k:
        copy.wait()
    load_v[0].wait()
    kv_all[0, 0, 1] = v_stage[0].T
    load_q[0].wait()
    pl.semaphore_wait(barrier, len(around))

    for way in range(2):
        start(kv_copy(0, way, 1))
    for j in range(1, nx):
        start(t_copy(j))
        start(q_copy(0, j))

    for h in range(1, heads):
        load_v[h].wait()
        kv_all[h, 0, 1] = v_stage[h].T
        for way in range(2):
            start(kv_copy(h, way, 1))
    for h in range(1, heads):
        load_q[h].wait()
        for j in range(1, nx):
            start(q_copy(h, j))
    for h in range(heads):
        start(w_copy(h))

    row = lax.broadcasted_iota(jnp.int32, (rows, HD), 0)
    column = lax.broadcasted_iota(jnp.int32, (rows, HD), 1)
    per = rows // BLOCK
    for s in range(ny):
        owner = lax.rem(y - s + ny, ny) * nx + x
        hot[s] = jnp.where(column == owner * per + row // BLOCK, 1.0, 0.0).astype(BF16)

    for j in range(1, nx):
        t_copy(j).wait_recv()
    for h in range(heads):
        for j in range(nx):
            for i in range(per):
                line = h * per + i
                wide = jnp.broadcast_to(t_all[j, line : line + 1, :], (BLOCK, HD))
                t_wide[h, j, i * BLOCK : (i + 1) * BLOCK, :] = wide.astype(BF16)

    def attend(h, slots, first):
        keys = jnp.concatenate(
            [jnp.concatenate([kv_all[h, s, 0], hot[s]], axis=1) for s in slots], axis=0
        )
        values = jnp.concatenate([kv_all[h, s, 1] for s in slots], axis=1)
        queries = jnp.concatenate(
            [q_all[h].reshape(nx * rows, HD), t_wide[h].reshape(nx * rows, HD)], axis=1
        )
        scores = lax.dot_general(
            keys, queries, (((1,), (1,)), ((), ())), preferred_element_type=F32
        )
        top = jnp.max(scores, axis=0, keepdims=True)
        if not first:
            old = top_now[h]
            top = jnp.maximum(top, old)
        probs = jnp.exp2((scores - top) * SCALE)
        total = jnp.sum(probs, axis=0, keepdims=True)
        mixed = jnp.dot(values, probs.astype(BF16), preferred_element_type=F32)
        if not first:
            fade = jnp.exp2((old - top) * SCALE)
            total = total + sum_now[h] * fade
            mixed = mixed + acc[h] * fade
        top_now[h] = top
        sum_now[h] = total
        acc[h] = mixed

    def share(h):
        for j in range(nx):
            lanes = slice(j * rows, (j + 1) * rows)
            if j == 0:
                st_out[h, j, 0:1, :] = top_now[h, :, lanes]
                st_out[h, j, 1:2, :] = sum_now[h, :, lanes]
                o_own[h] = acc[h, :, lanes]
            else:
                o_out[h, j, 0:HD] = acc[h, :, lanes].astype(BF16)
                line = lax.broadcasted_iota(jnp.int32, (16, rows), 0)
                packed = jnp.zeros((16, rows), F32)
                for k, rest in enumerate((top_now[h, :, lanes], sum_now[h, :, lanes])):
                    for i in range(3):
                        term = rest.astype(BF16).astype(F32)
                        packed = jnp.where(line == 3 * k + i, term, packed)
                        rest = rest - term
                o_out[h, j, HD : HD + 16] = packed.astype(BF16)
                start(o_copy(h, j))

    def merge(h):
        tops, sums = [st_out[h, 0, 0:1, :]], [st_out[h, 0, 1:2, :]]
        for j in range(1, nx):
            o_copy(h, j).wait_recv()
            packed = o_in[h, j, HD : HD + 16].astype(F32)
            tops.append(packed[0:1] + packed[1:2] + packed[2:3])
            sums.append(packed[3:4] + packed[4:5] + packed[5:6])
        top = functools.reduce(jnp.maximum, tops)
        weights = [jnp.exp2((t - top) * SCALE) for t in tops]
        denom = sum(w * s for w, s in zip(weights, sums))
        total = o_own[h] * weights[0]
        for j in range(1, nx):
            total = total + o_in[h, j, 0:HD].astype(F32) * weights[j]
        attended = (total / denom).T.astype(BF16)
        for i in range(2 * nz):
            place = slice(i // 2 * take, (i // 2 + 1) * take)
            a_out[h, i % 2, place, :] = attended[i * take : (i + 1) * take, :]
        for step in near + [0]:
            for flip in range(2):
                if flip or step:
                    start(a_copy(h, flip, step))
        a_all[h, 0, :, 0:HD] = a_out[h, core]

    arrived = set()

    def receive(h, flip, step):
        if (flip or step) and (h, flip, step) not in arrived:
            arrived.add((h, flip, step))
            a_copy(h, flip, step).wait_recv()

    def relay(h):
        if nd > 3:
            for flip in range(2):
                receive(h, flip, 1 if flip == 0 else nd - 1)
                start(a_relay(h, flip))

    def receive_keys(h, step):
        for way in range(2):
            kv_copy(h, way, step).wait_recv()
            if step < far:
                start(kv_copy(h, way, step + 1))

    last = heads - 1
    events = [(h, step) for step in range(1, far + 1) for h in range(heads)]
    for n, (h, step) in enumerate(events):
        receive_keys(h, step)
        if beside and n % 2 == 0 and n // 2 <= nz:
            pass_word(n // 2)
        if step == 1:
            for j in range(1, nx):
                q_copy(h, j).wait_recv()
        slots = [0] * (step == 1) + ([step, ny - step] if step < far else [far])
        attend(h, slots, step == 1)
        if step == far:
            share(h)
    for h in range(heads):
        merge(h)
    relay(0)
    for h in range(heads):
        load_w[h].wait()
        w_copy(h).wait_recv()

    lines, depth = nz * take, heads * 2 * HD
    weights = w_all[...].reshape(depth, w_all.shape[2])
    for step in [0] + near + list(range(2, nd - 1)):
        if near and step == near[0]:
            for h in range(1, heads):
                relay(h)
        for h in range(heads):
            for flip in range(2):
                receive(h, flip, step)
        rows_in = jnp.concatenate([a_all[h, step] for h in range(heads)], axis=1)
        mixed = jnp.dot(rows_in, weights, preferred_element_type=F32)
        part[step] = mixed.reshape(nz, take, mixed.shape[1])
        for j in range(1, nz):
            goal = lax.rem(z + j, nz)
            r_out[j, step] = part[step, goal].astype(BF16)
            start(r_copy(j, step))
    for step in range(nd):
        total = part[step, z]
        for j in range(1, nz):
            r_copy(j, step).wait_recv()
            total = total + r_in[j, step].astype(F32)
        out[lax.rem(d - step + nd, nd)] = total.astype(BF16)

    for copy in started:
        copy.wait_send()


def on_device(sizes, queries, keys, values, block_lists, block_counts, w_out):
    nx, ny, nz, nd = sizes
    rows, heads = queries.shape[1], queries.shape[2] // HD
    take, width = rows // (2 * nz), w_out.shape[1]
    dma = pltpu.SemaphoreType.DMA
    far = ny // 2
    return pl.pallas_call(
        functools.partial(fused, sizes),
        out_shape=jax.ShapeDtypeStruct((nd, take, width), BF16),
        in_specs=[pl.BlockSpec(memory_space=pl.ANY)] * 3
        + [pl.BlockSpec(memory_space=pltpu.SMEM)] * 2
        + [pl.BlockSpec(memory_space=pl.ANY)],
        out_specs=pl.BlockSpec(memory_space=pltpu.VMEM),
        scratch_shapes=[
            pltpu.VMEM((heads, nx, rows, HD), BF16),
            pltpu.VMEM((nx, 8, HD), F32),
            pltpu.VMEM((heads, nx, rows, HD), BF16),
            pltpu.VMEM((ny, rows, HD), BF16),
            pltpu.VMEM((heads, ny, 2, rows, HD), BF16),
            pltpu.VMEM((heads, rows, HD), BF16),
            pltpu.VMEM((heads, 1, nx * rows), F32),
            pltpu.VMEM((heads, 1, nx * rows), F32),
            pltpu.VMEM((heads, HD, nx * rows), F32),
            pltpu.VMEM((heads, HD, rows), F32),
            pltpu.VMEM((heads, nx, HD + 16, rows), BF16),
            pltpu.VMEM((heads, nx, HD + 16, rows), BF16),
            pltpu.VMEM((heads, nx, 8, rows), F32),
            pltpu.VMEM((heads, 2, nz * take, HD), BF16),
            pltpu.VMEM((heads, nd, nz * take, 2 * HD), BF16),
            pltpu.VMEM((heads, 2 * HD, width), BF16),
            pltpu.VMEM((nd, nz, take, width), F32),
            pltpu.VMEM((nz, nd, take, width), BF16),
            pltpu.VMEM((nz, nd, take, width), BF16),
            dma((4, heads)),
            dma((heads, 2, far)),
            dma((heads, ny + 1)),
            dma((heads, nx)),
            dma((heads, nx)),
            dma((nx,)),
            dma((nx,)),
            dma((heads, nx)),
            dma((heads, nx)),
            dma((heads, 2, nd)),
            dma((heads, 2, nd)),
            dma((heads,)),
            dma((heads,)),
            dma((nz, nd)),
            dma((nz, nd)),
            pltpu.SemaphoreType.REGULAR((nz, 2)),
        ],
        compiler_params=pltpu.CompilerParams(
            collective_id=0, has_side_effects=True, vmem_limit_bytes=60 * 2**20
        ),
        name="attention",
    )(queries, keys, values, block_lists, block_counts.transpose(0, 2, 1), w_out)


def solution(mesh):
    shape = mesh.shape
    sizes = (X_SIZE, shape["blk"] // X_SIZE, shape["uly"] // 2, shape["dp"])
    placed = (
        P("dp", "blk", "uly"),
        P("dp", "blk", "uly"),
        P("dp", "blk", "uly"),
        P("dp", "uly", "blk", None),
        P("dp", "uly", "blk"),
        P("uly", "dp"),
    )
    return jax.shard_map(
        functools.partial(on_device, sizes),
        mesh=mesh,
        in_specs=placed,
        out_specs=P(None, ("blk", "uly"), "dp"),
        check_vma=False,
    )
```
